128 devices in a mesh: ctx: 16 (over y, x_hi, core), tp: 8 (over x_lo, z).
Axes of the slice: x: 4 (x_hi: 2, x_lo: 2; x = x_hi * 2 + x_lo), y: 4, z: 4, core: 2. Of those that a mesh axis runs over, the one named last changes fastest.
Arguments:
- signal: bfloat16 [8192, 4096], P('ctx', 'tp'), may hold values from -6 to 6
- filter_taps: bfloat16 [8192, 4096], P('ctx', 'tp'), may hold values from -8 to 8
- skip_gain: float32 [4096], P('tp'), may hold values from -4 to 4
- upstream: bfloat16 [8192, 4096], P('ctx', 'tp'), may hold values from -6 to 6
Outputs:
- mixed: bfloat16 [8192, 4096], P('ctx', 'tp')
- signal_grad: bfloat16 [8192, 4096], P('ctx', 'tp')
- filter_grad: bfloat16 [8192, 4096], P('ctx', 'tp')
The draws below stay inside these ranges and needn't reach their ends.
All inputs are finite; a program needn't handle non-finite values.
Results may differ from the reference program's by a relative error of at most 0.011.
Values may be sent and summed in bfloat16 or wider, within the bound.
No kernel may reach another device: no remote copies, remote signals or barrier semaphores. Data moves between devices by JAX's collectives and lax.ppermute only.
A program may use at most 256 MiB of HBM per device.

```python
import math
import jax
import jax.numpy as jnp
from jax import lax

CH = 4096
SEQ_DEV = 512
FA = 32
FB = 16
SEQ = 8192
N_CTX = 16


def envelope_energy(decay_rate):
    return SEQ * (1.0 - jnp.exp(-2.0 * decay_rate)) / (2.0 * decay_rate)


def draw_filter_taps(key, part):
    key = jax.random.fold_in(key, 11)
    rate_key, slow_key, share_key, noise_key = jax.random.split(key, 4)
    log_rate = jax.random.uniform(rate_key, (CH,), jnp.float32, math.log(0.3), math.log(1000.0))
    log_slow = jax.random.uniform(slow_key, (CH,), jnp.float32, math.log(0.1), math.log(1.0))
    noise_draw = jnp.clip(jax.random.normal(noise_key, (SEQ, CH), jnp.float32), -5.0, 5.0)
    fast_rate = jnp.exp(log_rate)
    slow_rate = jnp.exp(log_slow)
    slow_share = jax.random.uniform(share_key, (CH,), jnp.float32, 0.3, 0.6)
    position = jnp.arange(SEQ, dtype=jnp.float32) / SEQ
    fast_env = jnp.exp(-position[:, None] * fast_rate[None, :]) * jnp.sqrt((1.0 - slow_share) / envelope_energy(fast_rate))[None, :]
    slow_env = jnp.exp(-position[:, None] * slow_rate[None, :]) * jnp.sqrt(slow_share / envelope_energy(slow_rate))[None, :]
    return (noise_draw * (fast_env + slow_env)).astype(jnp.bfloat16)


def block_scale(key, shape, cuts, smallest, largest):
    factor_of, own = 1.0, jax.random.fold_in(key, 6)
    for axis_at, parts in cuts:
        steps = jnp.exp(jax.random.uniform(jax.random.fold_in(own, axis_at), (parts,), jnp.float32, smallest / len(cuts), largest / len(cuts)))
        factor_of = factor_of * jnp.repeat(steps, shape[axis_at] // parts).reshape([-1 if axis == axis_at else 1 for axis in range(len(shape))])
    return factor_of


def centred(stream_key, extent, width, limit, cuts=(), kind=jnp.bfloat16):
    values = jax.random.normal(stream_key, extent, jnp.float32) * width
    if len(cuts) > 0:
        values = block_scale(stream_key, extent, cuts, -0.22, 0.18) * values
    return jnp.clip(values, min=-limit, max=limit).astype(kind)


def setup_inputs(seed: int = 0) -> dict:
    splits = jax.random.split(jax.random.key(seed), 5)
    signal = centred(splits[0], (SEQ, CH), 1.0, 6.0, ((0, 16), (1, 8)))
    filter_taps = draw_filter_taps(jax.random.fold_in(splits[4], 71), 0)
    skip_gain = centred(splits[2], (CH,), 1.0, 4.0, ((0, 8),), jnp.float32)
    upstream = centred(splits[3], (SEQ, CH), 1.0, 6.0, ((0, 16), (1, 8)))
    return {"signal": signal, "filter_taps": filter_taps, "skip_gain": skip_gain, "upstream": upstream}


TWO_PI = 2.0 * math.pi

def counting(count):
    return jnp.arange(count, dtype=jnp.int32)

def angle_tables(left_idx, right_idx, length):
    product = left_idx[:, None] * right_idx[None, :] % length
    angle_rad = product.astype(jnp.float32) * (TWO_PI / length)
    return (jnp.cos(angle_rad), jnp.sin(angle_rad))

def table_pair(left_idx, right_idx, length):
    cos_part, sin_part = angle_tables(left_idx, right_idx, length)
    cos_low = lax.optimization_barrier(cos_part.astype(jnp.bfloat16))
    sin_low = lax.optimization_barrier(sin_part.astype(jnp.bfloat16))
    return (cos_low.astype(jnp.float32), sin_low.astype(jnp.float32))

def mix(form, data, table):
    return jnp.einsum(form, data.astype(jnp.float32), table, precision=lax.Precision.HIGHEST)

def forward_q(slab_data, row_start, ctx_count):
    a_count = 2 * ctx_count
    length = a_count * SEQ_DEV
    q_cos, q_sin = table_pair(counting(ctx_count), counting(a_count), a_count)
    real_part = mix('kqrc,qa->karc', slab_data, q_cos)
    imag_part = -mix('kqrc,qa->karc', slab_data, q_sin)
    tw_cos, tw_sin = angle_tables(counting(a_count), row_start + counting(slab_data.shape[2]), length)
    tw_cos = tw_cos[None, :, :, None]
    tw_sin = tw_sin[None, :, :, None]
    return jnp.stack([real_part * tw_cos + imag_part * tw_sin, imag_part * tw_cos - real_part * tw_sin], axis=1).astype(jnp.bfloat16)

def forward_r(wave_data):
    kind_count, _, a_count, _, chan_count = wave_data.shape
    cell_data = wave_data.reshape(kind_count, 2, a_count, FA, FB, chan_count)
    a_cos, a_sin = table_pair(counting(FA), counting(FA), FA)
    real_in, imag_in = (cell_data[:, 0], cell_data[:, 1])
    real_part = mix('kasxc,sb->kabxc', real_in, a_cos) + mix('kasxc,sb->kabxc', imag_in, a_sin)
    imag_part = mix('kasxc,sb->kabxc', imag_in, a_cos) - mix('kasxc,sb->kabxc', real_in, a_sin)
    tw_cos, tw_sin = angle_tables(counting(FA), counting(FB), SEQ_DEV)
    tw_cos = tw_cos[None, None, :, :, None]
    tw_sin = tw_sin[None, None, :, :, None]
    sectioned = jnp.stack([real_part * tw_cos + imag_part * tw_sin, imag_part * tw_cos - real_part * tw_sin], axis=1).astype(jnp.bfloat16)
    b_cos, b_sin = table_pair(counting(FB), counting(FB), FB)
    real_in, imag_in = (sectioned[:, 0], sectioned[:, 1])
    real_part = mix('kabxc,xy->kabyc', real_in, b_cos) + mix('kabxc,xy->kabyc', imag_in, b_sin)
    imag_part = mix('kabxc,xy->kabyc', imag_in, b_cos) - mix('kabxc,xy->kabyc', real_in, b_sin)
    return jnp.stack([real_part, imag_part], axis=1).astype(jnp.bfloat16)

def spectral_product(spectra):
    values = spectra.astype(jnp.float32)
    sig_r, sig_i = (values[0, 0], values[0, 1])
    tap_r, tap_i = (values[1, 0], values[1, 1])
    up_r, up_i = (values[2, 0], values[2, 1])
    first_pair = jnp.stack([sig_r * tap_r - sig_i * tap_i, sig_r * tap_i + sig_i * tap_r])
    second_pair = jnp.stack([up_r * tap_r + up_i * tap_i, up_i * tap_r - up_r * tap_i])
    third_pair = jnp.stack([up_r * sig_r + up_i * sig_i, up_i * sig_r - up_r * sig_i])
    return jnp.stack([first_pair, second_pair, third_pair]).astype(jnp.bfloat16)

def inverse_r(product, a_start, ctx_count):
    kind_count, _, a_count, _, _, chan_count = product.shape
    length = 2 * ctx_count * SEQ_DEV
    b_cos, b_sin = table_pair(counting(FB), counting(FB), FB)
    real_in, imag_in = (product[:, 0], product[:, 1])
    real_part = mix('kabyc,xy->kabxc', real_in, b_cos) - mix('kabyc,xy->kabxc', imag_in, b_sin)
    imag_part = mix('kabyc,xy->kabxc', real_in, b_sin) + mix('kabyc,xy->kabxc', imag_in, b_cos)
    tw_cos, tw_sin = angle_tables(counting(FA), counting(FB), SEQ_DEV)
    tw_cos = tw_cos[None, None, :, :, None]
    tw_sin = tw_sin[None, None, :, :, None]
    sectioned = jnp.stack([real_part * tw_cos - imag_part * tw_sin, real_part * tw_sin + imag_part * tw_cos], axis=1).astype(jnp.bfloat16)
    a_cos, a_sin = table_pair(counting(FA), counting(FA), FA)
    real_in, imag_in = (sectioned[:, 0], sectioned[:, 1])
    real_part = mix('kabxc,sb->kasxc', real_in, a_cos) - mix('kabxc,sb->kasxc', imag_in, a_sin)
    imag_part = mix('kabxc,sb->kasxc', real_in, a_sin) + mix('kabxc,sb->kasxc', imag_in, a_cos)
    real_part = real_part.reshape(kind_count, a_count, SEQ_DEV, chan_count)
    imag_part = imag_part.reshape(kind_count, a_count, SEQ_DEV, chan_count)
    tw_cos, tw_sin = angle_tables(a_start + counting(a_count), counting(SEQ_DEV), length)
    tw_cos = tw_cos[None, :, :, None]
    tw_sin = tw_sin[None, :, :, None]
    return jnp.stack([real_part * tw_cos - imag_part * tw_sin, real_part * tw_sin + imag_part * tw_cos], axis=1).astype(jnp.bfloat16)

def inverse_q(band_data, ctx_count):
    a_count = 2 * ctx_count
    length = a_count * SEQ_DEV
    q_cos, q_sin = table_pair(counting(ctx_count), counting(a_count), a_count)
    real_sum = mix('karc,qa->kqrc', band_data[:, 0], q_cos) - mix('karc,qa->kqrc', band_data[:, 1], q_sin)
    return real_sum * (1.0 / length)

def finish(conv_sums, grid_data, gain_rows, grad_scale):
    signal_part = grid_data[0].astype(jnp.float32)
    upstream_part = grid_data[2].astype(jnp.float32)
    return jnp.stack([conv_sums[0] + gain_rows * signal_part, conv_sums[1] + gain_rows * upstream_part, conv_sums[2] * grad_scale]).astype(jnp.bfloat16)

def reference(signal, filter_taps, skip_gain, upstream):
    block_width = math.gcd(CH, 64)
    block_count = CH // block_width
    stacked = jnp.stack([signal, filter_taps, upstream]).reshape(3, SEQ, block_count, block_width).transpose(2, 0, 1, 3)
    gain_blocks = skip_gain.reshape(block_count, block_width)
    grad_scale = 1.0 / math.sqrt(SEQ)

    def one_block(block_pair):
        block_data, block_gain = block_pair
        grid_data = block_data.reshape(3, N_CTX, SEQ_DEV, block_width)
        wave_data = forward_q(grid_data, 0, N_CTX)
        band_data = inverse_r(spectral_product(forward_r(wave_data)), 0, N_CTX)
        conv_sums = inverse_q(band_data, N_CTX)
        return finish(conv_sums, grid_data, block_gain, grad_scale).reshape(3, SEQ, block_width)
    results = lax.map(one_block, (stacked, gain_blocks))
    results = results.transpose(1, 2, 0, 3).reshape(3, SEQ, CH)
    return (results[0], results[1], results[2])
```

```python
import math

import jax
import jax.numpy as jnp
import numpy as np
from jax import lax
from jax.experimental import pallas as pl
from jax.experimental.pallas import tpu as pltpu
from jax.sharding import PartitionSpec as P

SEQ_DEV = 512
CTX = 16
LANES = 128
CELLS = SEQ_DEV // LANES
GROUP = 16
KINDS = 3
LENGTH = CTX * SEQ_DEV
VMEM_BYTES = 56 * 1024 * 1024


def slab_tables():
    slab = np.arange(CTX)
    tables = []
    for cell in range(CELLS):
        angle = 2.0 * math.pi * np.outer(slab + 0.25, CELLS * slab + cell) / (CTX * CELLS)
        both = np.concatenate([np.cos(angle), -np.sin(angle)])
        tables.append(np.kron(both, np.eye(GROUP)))
    return np.stack(tables)


def lane_table():
    spot = np.arange(LANES)
    angle = 2.0 * math.pi * (np.outer(spot, spot) % LANES) / LANES
    cos_part, sin_part = np.cos(angle), np.sin(angle)
    return np.block([[cos_part, -sin_part], [sin_part, cos_part]])


def twist_tables():
    rate = np.arange(CTX)[None, :] + 0.25 + CTX * np.arange(CELLS)[:, None]
    angle = 2.0 * math.pi * rate[:, :, None] * np.arange(LANES) / LENGTH
    return np.stack([np.cos(angle), np.sin(angle)])


def to_channels(sig_ref, tap_ref, up_ref, out_ref):
    for kind, ref in enumerate((sig_ref, tap_ref, up_ref)):
        out_ref[:, kind] = ref[...].T.reshape(out_ref.shape[0], out_ref.shape[2], SEQ_DEV)


def to_positions(in_ref, mix_ref, sig_ref, tap_ref):
    for kind, ref in enumerate((mix_ref, sig_ref, tap_ref)):
        ref[...] = in_ref[:, kind].reshape(LANES, SEQ_DEV).T


def convolve(
    x_ref, gain_ref, slab_ref, back_ref, lane_ref, unlane_ref, twist_ref, out_ref, wave, band, spec, coef
):
    groups = x_ref.shape[2] // GROUP
    half = CTX * GROUP
    chans = x_ref.shape[2]

    for cell in range(CELLS):
        lanes = slice(cell * LANES, (cell + 1) * LANES)
        data = jnp.concatenate(
            [
                x_ref[:, kind, g * GROUP : (g + 1) * GROUP, lanes].reshape(half, LANES)
                for kind in range(KINDS)
                for g in range(groups)
            ],
            axis=1,
        )
        wave[cell] = jnp.dot(slab_ref[cell], data, preferred_element_type=jnp.float32)

    for part in range(KINDS * groups):
        lanes = slice(part * LANES, (part + 1) * LANES)

        def forward(a, carry, part=part, lanes=lanes):
            rows = pl.ds(pl.multiple_of(a * GROUP, GROUP), GROUP)
            low = pl.ds(pl.multiple_of(half + a * GROUP, GROUP), GROUP)
            r0, r1, r2, r3 = (wave[cell, rows, lanes] for cell in range(CELLS))
            i0, i1, i2, i3 = (wave[cell, low, lanes] for cell in range(CELLS))
            ra, rb, rc, rd = r0 + r2, r0 - r2, r1 + r3, r1 - r3
            ia, ib, ic, id_ = i0 + i2, i0 - i2, i1 + i3, i1 - i3
            real = (ra + rc, rb + id_, ra - rc, rb - id_)
            imag = (ia + ic, ib - rd, ia - ic, ib + rd)
            for b in range(CELLS):
                cos_part = twist_ref[0, b, pl.ds(a, 1), :]
                sin_part = twist_ref[1, b, pl.ds(a, 1), :]
                band[part, b, rows, :LANES] = (real[b] * cos_part + imag[b] * sin_part).astype(jnp.bfloat16)
                band[part, b, rows, LANES:] = (imag[b] * cos_part - real[b] * sin_part).astype(jnp.bfloat16)
            return carry

        lax.fori_loop(0, CTX, forward, 0, unroll=4)

    def middle(step, carry):
        g, b = step // CELLS, lax.rem(step, CELLS)
        for kind in range(KINDS):
            spec[kind] = jnp.dot(band[kind * groups + g, b], lane_ref[...], preferred_element_type=jnp.float32)

        def product(row, inner):
            rows = pl.ds(pl.multiple_of(row * GROUP, GROUP), GROUP)
            sig_r, sig_i = spec[0, rows, :LANES], spec[0, rows, LANES:]
            tap_r, tap_i = spec[1, rows, :LANES], spec[1, rows, LANES:]
            up_r, up_i = spec[2, rows, :LANES], spec[2, rows, LANES:]
            pairs = (
                (sig_r * tap_r - sig_i * tap_i, sig_r * tap_i + sig_i * tap_r),
                (up_r * tap_r + up_i * tap_i, up_i * tap_r - up_r * tap_i),
                (up_r * sig_r + up_i * sig_i, up_i * sig_r - up_r * sig_i),
            )
            for kind, (real, imag) in enumerate(pairs):
                band[kind * groups + g, b, rows, :LANES] = real.astype(jnp.bfloat16)
                band[kind * groups + g, b, rows, LANES:] = imag.astype(jnp.bfloat16)
            return inner

        lax.fori_loop(0, half // GROUP, product, 0, unroll=4)
        for kind in range(KINDS):
            wave_part = jnp.dot(
                band[kind * groups + g, b], unlane_ref[...], preferred_element_type=jnp.float32
            )
            back = kind * groups + g
            coef[back, b] = wave_part
        return carry

    lax.fori_loop(0, groups * CELLS, middle, 0)

    for part in range(KINDS * groups):
        lanes = slice(part * LANES, (part + 1) * LANES)

        def backward(a, carry, part=part, lanes=lanes):
            rows = pl.ds(pl.multiple_of(a * GROUP, GROUP), GROUP)
            low = pl.ds(pl.multiple_of(half + a * GROUP, GROUP), GROUP)
            real, imag = [], []
            for b in range(CELLS):
                cos_part = twist_ref[0, b, pl.ds(a, 1), :]
                sin_part = twist_ref[1, b, pl.ds(a, 1), :]
                real_in, imag_in = coef[part, b, rows, :LANES], coef[part, b, rows, LANES:]
                real.append(real_in * cos_part - imag_in * sin_part)
                imag.append(imag_in * cos_part + real_in * sin_part)
            ra, rb, rc, rd = real[0] + real[2], real[0] - real[2], real[1] + real[3], real[1] - real[3]
            ia, ib, ic, id_ = imag[0] + imag[2], imag[0] - imag[2], imag[1] + imag[3], imag[1] - imag[3]
            real = (ra + rc, rb - id_, ra - rc, rb + id_)
            imag = (ia + ic, ib + rd, ia - ic, ib - rd)
            for cell in range(CELLS):
                wave[cell, rows, lanes] = real[cell]
                wave[cell, low, lanes] = imag[cell]
            return carry

        lax.fori_loop(0, CTX, backward, 0, unroll=4)

    pick = lax.broadcasted_iota(jnp.int32, (chans, gain_ref.shape[1]), 1)
    own = lax.axis_index("ctx") * chans + lax.broadcasted_iota(jnp.int32, (chans, gain_ref.shape[1]), 0)
    gain = jnp.sum(jnp.where(pick == own, gain_ref[...], 0.0), axis=1, keepdims=True)
    grad_scale = 1.0 / math.sqrt(LENGTH)

    for cell in range(CELLS):
        lanes = slice(cell * LANES, (cell + 1) * LANES)
        sums = jnp.dot(
            back_ref[cell], wave[cell].astype(jnp.bfloat16), preferred_element_type=jnp.float32
        ) * (1.0 / LENGTH)
        for kind in range(KINDS):
            for g in range(groups):
                part = kind * groups + g
                chan = slice(g * GROUP, (g + 1) * GROUP)
                conv = sums[:, part * LANES : (part + 1) * LANES].reshape(CTX, GROUP, LANES)
                if kind < 2:
                    direct = x_ref[:, 2 * kind, chan, lanes].astype(jnp.float32)
                    conv = conv + gain[chan][None] * direct
                else:
                    conv = conv * grad_scale
                out_ref[:, kind, chan, lanes] = conv.astype(jnp.bfloat16)


def local(signal, filter_taps, skip_gain, upstream):
    ctx_count = lax.axis_size("ctx")
    chan_count = signal.shape[1]
    share = chan_count // ctx_count
    per_block = LANES // share
    groups = share // GROUP
    parts = KINDS * groups
    bf16, f32 = jnp.bfloat16, jnp.float32
    params = pltpu.CompilerParams(vmem_limit_bytes=VMEM_BYTES)
    slab_shape = (ctx_count, KINDS, share, SEQ_DEV)
    column = pl.BlockSpec((SEQ_DEV, LANES), lambda i: (0, i))
    piece = pl.BlockSpec((per_block, KINDS, share, SEQ_DEV), lambda i: (i, 0, 0, 0))

    pieces = pl.pallas_call(
        to_channels,
        grid=(chan_count // LANES,),
        in_specs=[column] * 3,
        out_specs=piece,
        out_shape=jax.ShapeDtypeStruct(slab_shape, bf16),
        compiler_params=params,
    )(signal, filter_taps, upstream)
    whole = lax.all_to_all(pieces, "ctx", split_axis=0, concat_axis=0, tiled=True)

    slabs = slab_tables()
    lanes = lane_table()
    half = CTX * GROUP
    results = pl.pallas_call(
        convolve,
        out_shape=jax.ShapeDtypeStruct(slab_shape, bf16),
        scratch_shapes=[
            pltpu.VMEM((CELLS, 2 * half, parts * LANES), f32),
            pltpu.VMEM((parts, CELLS, half, 2 * LANES), bf16),
            pltpu.VMEM((KINDS, half, 2 * LANES), f32),
            pltpu.VMEM((parts, CELLS, half, 2 * LANES), f32),
        ],
        compiler_params=params,
    )(
        whole,
        skip_gain.reshape(1, chan_count),
        jnp.asarray(slabs, bf16),
        jnp.asarray(slabs.transpose(0, 2, 1), bf16),
        jnp.asarray(lanes, bf16),
        jnp.asarray(lanes.T, bf16),
        jnp.asarray(twist_tables(), f32),
    )
    returned = lax.all_to_all(results, "ctx", split_axis=0, concat_axis=0, tiled=True)
    return pl.pallas_call(
        to_positions,
        grid=(chan_count // LANES,),
        in_specs=[piece],
        out_specs=[column] * 3,
        out_shape=[jax.ShapeDtypeStruct((SEQ_DEV, chan_count), bf16)] * 3,
        compiler_params=params,
    )(returned)


def solution(mesh):
    in_specs = (P("ctx", "tp"), P("ctx", "tp"), P("tp"), P("ctx", "tp"))
    out_specs = (P("ctx", "tp"), P("ctx", "tp"), P("ctx", "tp"))
    return jax.shard_map(local, mesh=mesh, in_specs=in_specs, out_specs=out_specs, check_vma=False)
```

```python
import functools
import math

import jax
import jax.numpy as jnp
import numpy as np
from jax import lax
from jax.experimental import pallas as pl
from jax.experimental.pallas import tpu as pltpu
from jax.sharding import PartitionSpec as P

SEQ_DEV = 512
LANES = 128
CELLS = SEQ_DEV // LANES
QUAD = 4
KINDS = 3
STEP_GROUPS = 4
FILL_BYTES = 58 * 1024 * 1024
ROOM_BYTES = 30 * 1024 * 1024
BF16 = jnp.bfloat16
F32 = jnp.float32


def wide_table(points):
    spot = np.arange(points)
    angle = 2.0 * math.pi * np.outer(spot + 0.25, spot) / points
    return np.kron(np.concatenate([np.cos(angle), -np.sin(angle)]), np.eye(QUAD))


def lane_table():
    spot = np.arange(LANES)
    angle = 2.0 * math.pi * (np.outer(spot, spot) % LANES) / LANES
    cos_part, sin_part = np.cos(angle), np.sin(angle)
    return np.block([[cos_part, -sin_part], [sin_part, cos_part]])


def twist_tables(points):
    angle = 2.0 * math.pi * np.outer(np.arange(points) + 0.25, np.arange(LANES)) / (points * LANES)
    return np.repeat(np.stack([np.cos(angle), np.sin(angle)]), QUAD, axis=1)


def shuffle(shape, row_axis):
    row = lax.broadcasted_iota(jnp.int32, shape, row_axis)
    col = lax.broadcasted_iota(jnp.int32, shape, 1 - row_axis)
    wanted = row // (QUAD * CELLS) * QUAD + row % QUAD + row // QUAD % CELLS * LANES
    return (col == wanted).astype(F32).astype(BF16)


def to_channels(sig_ref, tap_ref, up_ref, out_ref, table, data, sems):
    blocks = data.shape[0]
    per_block = out_ref.shape[0] // blocks

    def fetch(kind, block):
        source = (sig_ref, tap_ref, up_ref)[kind].at[:, pl.ds(block * LANES, LANES)]
        return pltpu.make_async_copy(source, data.at[block, kind], sems.at[block, kind])

    for block in range(blocks):
        for kind in range(KINDS):
            fetch(kind, block).start()
    table[...] = shuffle(table.shape, 0)
    for block in range(blocks):
        for kind in range(KINDS):
            fetch(kind, block).wait()
        wide = [
            jnp.concatenate([data[block, kind, c * LANES : (c + 1) * LANES, :] for c in range(CELLS)], axis=1)
            for kind in range(KINDS)
        ]
        turned = lax.dot_general(
            table[...], jnp.concatenate(wide, axis=0), (((1,), (1,)), ((), ())), preferred_element_type=F32
        ).astype(BF16)
        for kind in range(KINDS):
            piece = turned[:, kind * LANES : (kind + 1) * LANES]
            out_ref[block * per_block : (block + 1) * per_block, kind] = piece.reshape(
                per_block, *out_ref.shape[2:]
            )


def to_positions(in_ref, mix_ref, sig_ref, tap_ref, table, data, sems):
    blocks = data.shape[0]
    per_block = in_ref.shape[0] // blocks

    def flush(kind, block):
        target = (mix_ref, sig_ref, tap_ref)[kind].at[:, pl.ds(block * LANES, LANES)]
        return pltpu.make_async_copy(data.at[block, kind], target, sems.at[block, kind])

    table[...] = shuffle(table.shape, 0)
    for block in range(blocks):
        for kind in range(KINDS):
            piece = in_ref[block * per_block : (block + 1) * per_block, kind].reshape(CELLS * LANES, LANES)
            turned = lax.dot_general(
                piece, table[...], (((0,), (0,)), ((), ())), preferred_element_type=F32
            ).astype(BF16)
            for c in range(CELLS):
                data[block, kind, c * LANES : (c + 1) * LANES, :] = turned[:, c * LANES : (c + 1) * LANES]
            flush(kind, block).start()
    for block in range(blocks):
        for kind in range(KINDS):
            flush(kind, block).wait()


def convolve(x_ref, gain_ref, wide_ref, back_ref, lane_ref, unlane_ref, twist_ref, out_ref, gains):
    slabs, _, groups, cell_rows, _ = x_ref.shape
    rows = slabs * cell_rows
    grad_scale = 1.0 / math.sqrt(slabs * SEQ_DEV)

    shape = (groups * cell_rows, gain_ref.shape[1])
    line = lax.broadcasted_iota(jnp.int32, shape, 0)
    own = lax.axis_index("ctx") * (groups * QUAD) + line // cell_rows * QUAD + line % QUAD
    picked = jnp.where(lax.broadcasted_iota(jnp.int32, shape, 1) == own, gain_ref[...], 0.0)
    gains[...] = jnp.broadcast_to(jnp.sum(picked, axis=1, keepdims=True), gains.shape)

    def step(index, carry):
        units = [(kind, index * STEP_GROUPS + j) for j in range(STEP_GROUPS) for kind in range(KINDS)]
        data = jnp.concatenate([x_ref[:, kind, g].reshape(rows, LANES) for kind, g in units], axis=1)
        wave = jnp.dot(wide_ref[...], data, preferred_element_type=F32)
        spectra = []
        for u in range(len(units)):
            cols = slice(u * LANES, (u + 1) * LANES)
            real, imag = wave[:rows, cols], wave[rows:, cols]
            cos_part, sin_part = twist_ref[0], twist_ref[1]
            band = [real * cos_part + imag * sin_part, imag * cos_part - real * sin_part]
            band = jnp.concatenate([part.astype(BF16) for part in band], axis=1)
            spectra.append(jnp.dot(band, lane_ref[...], preferred_element_type=F32))
        bands = []
        for j in range(STEP_GROUPS):
            (sig_r, sig_i), (tap_r, tap_i), (up_r, up_i) = (
                (part[:, :LANES], part[:, LANES:]) for part in spectra[KINDS * j : KINDS * (j + 1)]
            )
            pairs = (
                (sig_r * tap_r - sig_i * tap_i, sig_r * tap_i + sig_i * tap_r),
                (up_r * tap_r + up_i * tap_i, up_i * tap_r - up_r * tap_i),
                (up_r * sig_r + up_i * sig_i, up_i * sig_r - up_r * sig_i),
            )
            for pair in pairs:
                product = jnp.concatenate([part.astype(BF16) for part in pair], axis=1)
                coef = jnp.dot(product, unlane_ref[...], preferred_element_type=F32)
                real, imag = coef[:, :LANES], coef[:, LANES:]
                cos_part, sin_part = twist_ref[0], twist_ref[1]
                band = [real * cos_part - imag * sin_part, imag * cos_part + real * sin_part]
                bands.append(jnp.concatenate([part.astype(BF16) for part in band], axis=0))
        sums = jnp.dot(back_ref[...], jnp.concatenate(bands, axis=1), preferred_element_type=F32)
        for u, (kind, g) in enumerate(units):
            conv = sums[:, u * LANES : (u + 1) * LANES].reshape(slabs, cell_rows, LANES)
            if kind < 2:
                gain = gains[pl.ds(pl.multiple_of(g * cell_rows, cell_rows), cell_rows), :]
                conv = conv + gain[None] * x_ref[:, 2 * kind, g].astype(F32)
            else:
                conv = conv * grad_scale
            out_ref[:, kind, g] = conv.astype(BF16)
        return carry

    lax.fori_loop(0, groups // STEP_GROUPS, step, 0)


def local(signal, filter_taps, skip_gain, upstream):
    ctx_count = lax.axis_size("ctx")
    chan_count = signal.shape[1]
    groups = chan_count // ctx_count // QUAD
    blocks = chan_count // LANES
    points = ctx_count * CELLS
    pieces = jax.ShapeDtypeStruct((ctx_count, KINDS, groups, CELLS * QUAD, LANES), BF16)
    hbm = pl.BlockSpec(memory_space=pltpu.HBM)
    turning = [
        pltpu.VMEM((CELLS * LANES, CELLS * LANES), BF16),
        pltpu.VMEM((blocks, KINDS, SEQ_DEV, LANES), BF16),
        pltpu.SemaphoreType.DMA((blocks, KINDS)),
    ]
    exchange = functools.partial(lax.all_to_all, axis_name="ctx", split_axis=0, concat_axis=0, tiled=True)

    sent = pl.pallas_call(
        to_channels,
        in_specs=[hbm] * 3,
        out_shape=pieces,
        scratch_shapes=turning,
        compiler_params=pltpu.CompilerParams(vmem_limit_bytes=FILL_BYTES),
        name="to_channels",
    )(signal, filter_taps, upstream)
    whole = exchange(sent)

    wide, lanes = wide_table(points), lane_table()
    results = pl.pallas_call(
        convolve,
        out_shape=pieces,
        scratch_shapes=[pltpu.VMEM((groups * CELLS * QUAD, LANES), F32)],
        compiler_params=pltpu.CompilerParams(vmem_limit_bytes=ROOM_BYTES),
        name="convolve",
    )(
        whole,
        skip_gain.reshape(1, chan_count),
        jnp.asarray(wide, BF16),
        jnp.asarray(wide.T / (points * LANES), BF16),
        jnp.asarray(lanes, BF16),
        jnp.asarray(lanes.T, BF16),
        jnp.asarray(twist_tables(points), F32),
    )
    returned = exchange(results)
    return pl.pallas_call(
        to_positions,
        out_specs=[hbm] * 3,
        out_shape=[jax.ShapeDtypeStruct((SEQ_DEV, chan_count), BF16)] * 3,
        scratch_shapes=turning,
        compiler_params=pltpu.CompilerParams(vmem_limit_bytes=ROOM_BYTES),
        name="to_positions",
    )(returned)


def solution(mesh):
    in_specs = (P("ctx", "tp"), P("ctx", "tp"), P("tp"), P("ctx", "tp"))
    out_specs = (P("ctx", "tp"), P("ctx", "tp"), P("ctx", "tp"))
    return jax.shard_map(local, mesh=mesh, in_specs=in_specs, out_specs=out_specs, check_vma=False)
```

```python
import functools
import math

import jax
import jax.numpy as jnp
import numpy as np
from jax import lax
from jax.experimental import pallas as pl
from jax.experimental.pallas import tpu as pltpu
from jax.sharding import PartitionSpec as P

SEQ_DEV = 512
LANES = 128
CELLS = SEQ_DEV // LANES
QUAD = 4
KINDS = 3
STEP_GROUPS = 2
FILL_BYTES = 58 * 1024 * 1024
ROOM_BYTES = 32 * 1024 * 1024
BF16 = jnp.bfloat16
F32 = jnp.float32


def wide_table(points):
    spot = np.arange(points)
    angle = 2.0 * math.pi * np.outer(spot + 0.25, spot) / points
    return np.kron(np.concatenate([np.cos(angle), -np.sin(angle)]), np.eye(QUAD))


def lane_table():
    spot = np.arange(LANES)
    angle = 2.0 * math.pi * (np.outer(spot, spot) % LANES) / LANES
    cos_part, sin_part = np.cos(angle), np.sin(angle)
    return np.block([[cos_part, -sin_part], [sin_part, cos_part]])


def twist_tables(points):
    angle = 2.0 * math.pi * np.outer(np.arange(points) + 0.25, np.arange(LANES)) / (points * LANES)
    return np.repeat(np.stack([np.cos(angle), np.sin(angle)]), QUAD, axis=1)


def shuffle(shape, row_axis):
    row = lax.broadcasted_iota(jnp.int32, shape, row_axis)
    col = lax.broadcasted_iota(jnp.int32, shape, 1 - row_axis)
    wanted = row // (QUAD * CELLS) * QUAD + row % QUAD + row // QUAD % CELLS * LANES
    return (col == wanted).astype(F32).astype(BF16)


def to_channels(sig_ref, tap_ref, up_ref, out_ref, table, data, turned, sems, out_sems):
    blocks = data.shape[0]
    per_block = out_ref.shape[0] // blocks

    def fetch(kind, block):
        source = (sig_ref, tap_ref, up_ref)[kind].at[:, pl.ds(block * LANES, LANES)]
        return pltpu.make_async_copy(source, data.at[block, kind], sems.at[block, kind])

    def flush(block):
        devices = pl.ds(block * per_block, per_block)
        return pltpu.make_async_copy(turned.at[devices], out_ref.at[devices], out_sems.at[block])

    for block in range(blocks):
        for kind in range(KINDS):
            fetch(kind, block).start()
    table[...] = shuffle(table.shape, 0)

    def turn(block, carry):
        for kind in range(KINDS):
            fetch(kind, block).wait()
        wide = [
            jnp.concatenate([data[block, kind, c * LANES : (c + 1) * LANES, :] for c in range(CELLS)], axis=1)
            for kind in range(KINDS)
        ]
        found = lax.dot_general(
            table[...], jnp.concatenate(wide, axis=0), (((1,), (1,)), ((), ())), preferred_element_type=F32
        ).astype(BF16)
        for kind in range(KINDS):
            piece = found[:, kind * LANES : (kind + 1) * LANES]
            turned[pl.ds(block * per_block, per_block), kind] = piece.reshape(per_block, *out_ref.shape[2:])
        flush(block).start()
        return carry

    lax.fori_loop(0, blocks, turn, 0)
    for block in range(blocks):
        flush(block).wait()


def to_positions(in_ref, mix_ref, sig_ref, tap_ref, table, data, sems):
    blocks = data.shape[0]
    per_block = in_ref.shape[0] // blocks

    def flush(kind, block):
        target = (mix_ref, sig_ref, tap_ref)[kind].at[:, pl.ds(block * LANES, LANES)]
        return pltpu.make_async_copy(data.at[block, kind], target, sems.at[block, kind])

    table[...] = shuffle(table.shape, 0)
    for block in range(blocks):
        for kind in range(KINDS):
            piece = in_ref[block * per_block : (block + 1) * per_block, kind].reshape(CELLS * LANES, LANES)
            turned = lax.dot_general(
                piece, table[...], (((0,), (0,)), ((), ())), preferred_element_type=F32
            ).astype(BF16)
            for c in range(CELLS):
                data[block, kind, c * LANES : (c + 1) * LANES, :] = turned[:, c * LANES : (c + 1) * LANES]
            flush(kind, block).start()
    for block in range(blocks):
        for kind in range(KINDS):
            flush(kind, block).wait()


def convolve(x_ref, gain_ref, wide_ref, back_ref, lane_ref, unlane_ref, twist_ref, out_ref, gains):
    slabs, _, groups, cell_rows, _ = x_ref.shape
    rows = slabs * cell_rows
    grad_scale = 1.0 / math.sqrt(slabs * SEQ_DEV)

    shape = (groups * cell_rows, gain_ref.shape[1])
    line = lax.broadcasted_iota(jnp.int32, shape, 0)
    own = lax.axis_index("ctx") * (groups * QUAD) + line // cell_rows * QUAD + line % QUAD
    picked = jnp.where(lax.broadcasted_iota(jnp.int32, shape, 1) == own, gain_ref[...], 0.0)
    gains[...] = jnp.broadcast_to(jnp.sum(picked, axis=1, keepdims=True), gains.shape)

    for start in range(0, groups, STEP_GROUPS):
        units = [(kind, start + j) for j in range(STEP_GROUPS) for kind in range(KINDS)]
        data = jnp.concatenate([x_ref[:, kind, g].reshape(rows, LANES) for kind, g in units], axis=1)
        wave = jnp.dot(wide_ref[...], data, preferred_element_type=F32)
        spectra = []
        for u in range(len(units)):
            cols = slice(u * LANES, (u + 1) * LANES)
            real, imag = wave[:rows, cols], wave[rows:, cols]
            cos_part, sin_part = twist_ref[0], twist_ref[1]
            band = [real * cos_part + imag * sin_part, imag * cos_part - real * sin_part]
            band = jnp.concatenate([part.astype(BF16) for part in band], axis=1)
            spectra.append(jnp.dot(band, lane_ref[...], preferred_element_type=F32))
        bands = []
        for j in range(STEP_GROUPS):
            (sig_r, sig_i), (tap_r, tap_i), (up_r, up_i) = (
                (part[:, :LANES], part[:, LANES:]) for part in spectra[KINDS * j : KINDS * (j + 1)]
            )
            pairs = (
                (sig_r * tap_r - sig_i * tap_i, sig_r * tap_i + sig_i * tap_r),
                (up_r * tap_r + up_i * tap_i, up_i * tap_r - up_r * tap_i),
                (up_r * sig_r + up_i * sig_i, up_i * sig_r - up_r * sig_i),
            )
            for pair in pairs:
                product = jnp.concatenate([part.astype(BF16) for part in pair], axis=1)
                coef = jnp.dot(product, unlane_ref[...], preferred_element_type=F32)
                real, imag = coef[:, :LANES], coef[:, LANES:]
                cos_part, sin_part = twist_ref[0], twist_ref[1]
                band = [real * cos_part - imag * sin_part, imag * cos_part + real * sin_part]
                bands.append(jnp.concatenate([part.astype(BF16) for part in band], axis=0))
        sums = jnp.dot(back_ref[...], jnp.concatenate(bands, axis=1), preferred_element_type=F32)
        for u, (kind, g) in enumerate(units):
            conv = sums[:, u * LANES : (u + 1) * LANES].reshape(slabs, cell_rows, LANES)
            if kind < 2:
                gain = gains[g * cell_rows : (g + 1) * cell_rows, :]
                conv = conv + gain[None] * x_ref[:, 2 * kind, g].astype(F32)
            else:
                conv = conv * grad_scale
            out_ref[:, kind, g] = conv.astype(BF16)


def local(signal, filter_taps, skip_gain, upstream):
    ctx_count = lax.axis_size("ctx")
    chan_count = signal.shape[1]
    groups = chan_count // ctx_count // QUAD
    blocks = chan_count // LANES
    points = ctx_count * CELLS
    pieces = jax.ShapeDtypeStruct((ctx_count, KINDS, groups, CELLS * QUAD, LANES), BF16)
    hbm = pl.BlockSpec(memory_space=pltpu.HBM)
    turning = [
        pltpu.VMEM((CELLS * LANES, CELLS * LANES), BF16),
        pltpu.VMEM((blocks, KINDS, SEQ_DEV, LANES), BF16),
        pltpu.SemaphoreType.DMA((blocks, KINDS)),
    ]
    exchange = functools.partial(lax.all_to_all, axis_name="ctx", split_axis=0, concat_axis=0, tiled=True)

    sent = pl.pallas_call(
        to_channels,
        in_specs=[hbm] * 3,
        out_specs=hbm,
        out_shape=pieces,
        scratch_shapes=turning[:2]
        + [pltpu.VMEM(pieces.shape, BF16), turning[2], pltpu.SemaphoreType.DMA((blocks,))],
        compiler_params=pltpu.CompilerParams(vmem_limit_bytes=FILL_BYTES),
        name="to_channels",
    )(signal, filter_taps, upstream)
    whole = exchange(sent)

    wide, lanes = wide_table(points), lane_table()
    results = pl.pallas_call(
        convolve,
        out_shape=pieces,
        scratch_shapes=[pltpu.VMEM((groups * CELLS * QUAD, LANES), F32)],
        compiler_params=pltpu.CompilerParams(vmem_limit_bytes=ROOM_BYTES),
        name="convolve",
    )(
        whole,
        skip_gain.reshape(1, chan_count),
        jnp.asarray(wide, BF16),
        jnp.asarray(wide.T / (points * LANES), BF16),
        jnp.asarray(lanes, BF16),
        jnp.asarray(lanes.T, BF16),
        jnp.asarray(twist_tables(points), F32),
    )
    returned = exchange(results)
    return pl.pallas_call(
        to_positions,
        out_specs=[hbm] * 3,
        out_shape=[jax.ShapeDtypeStruct((SEQ_DEV, chan_count), BF16)] * 3,
        scratch_shapes=turning,
        compiler_params=pltpu.CompilerParams(vmem_limit_bytes=ROOM_BYTES),
        name="to_positions",
    )(returned)


def solution(mesh):
    in_specs = (P("ctx", "tp"), P("ctx", "tp"), P("tp"), P("ctx", "tp"))
    out_specs = (P("ctx", "tp"), P("ctx", "tp"), P("ctx", "tp"))
    return jax.shard_map(local, mesh=mesh, in_specs=in_specs, out_specs=out_specs, check_vma=False)
```

```python
import functools
import math

import jax
import jax.numpy as jnp
import numpy as np
from jax import lax
from jax.experimental import pallas as pl
from jax.experimental.pallas import tpu as pltpu
from jax.sharding import PartitionSpec as P

SEQ_DEV = 512
LANES = 128
CELLS = SEQ_DEV // LANES
QUAD = 4
PAIR = 2
SPLITS = CELLS // PAIR
KINDS = 3
STEP_GROUPS = 2
FILL_BYTES = 58 * 1024 * 1024
ROOM_BYTES = 32 * 1024 * 1024
BF16 = jnp.bfloat16
F32 = jnp.float32


def wide_table(points):
    spot = np.arange(points)
    angle = 2.0 * math.pi * np.outer(spot + 0.25, spot) / points
    return np.kron(np.concatenate([np.cos(angle), -np.sin(angle)]), np.eye(QUAD))


def lane_table():
    spot = np.arange(LANES)
    angle = 2.0 * math.pi * (np.outer(spot, spot) % LANES) / LANES
    cos_part, sin_part = np.cos(angle), np.sin(angle)
    return np.block([[cos_part, -sin_part], [sin_part, cos_part]])


def twist_tables(points):
    angle = 2.0 * math.pi * np.outer(np.arange(points) + 0.25, np.arange(LANES)) / (points * LANES)
    return np.repeat(np.stack([np.cos(angle), np.sin(angle)]), QUAD, axis=1)


def shuffle(shape, row_axis):
    row = lax.broadcasted_iota(jnp.int32, shape, row_axis)
    col = lax.broadcasted_iota(jnp.int32, shape, 1 - row_axis)
    wanted = row // (QUAD * PAIR) * QUAD + row % QUAD + row // QUAD % PAIR * LANES
    return (col == wanted).astype(F32).astype(BF16)


def to_channels(sig_ref, tap_ref, up_ref, out_ref, table, data, turned, sems, out_sems):
    blocks = data.shape[0]
    per_block = out_ref.shape[0] // blocks

    def fetch(kind, block):
        source = (sig_ref, tap_ref, up_ref)[kind].at[:, pl.ds(block * LANES, LANES)]
        return pltpu.make_async_copy(source, data.at[block, kind], sems.at[block, kind])

    def flush(block):
        devices = pl.ds(block * per_block, per_block)
        return pltpu.make_async_copy(turned.at[devices], out_ref.at[devices], out_sems.at[block])

    for block in range(blocks):
        for kind in range(KINDS):
            fetch(kind, block).start()
    table[...] = shuffle(table.shape, 0)

    def turn(block, carry):
        for kind in range(KINDS):
            fetch(kind, block).wait()
        halves = []
        for split in range(SPLITS):
            wide = [
                jnp.concatenate(
                    [data[block, kind, c * LANES : (c + 1) * LANES, :] for c in range(split * PAIR, (split + 1) * PAIR)],
                    axis=1,
                )
                for kind in range(KINDS)
            ]
            found = lax.dot_general(
                table[...], jnp.concatenate(wide, axis=0), (((1,), (1,)), ((), ())), preferred_element_type=F32
            )
            halves.append(found.reshape(-1, PAIR * QUAD, KINDS * LANES))
        found = jnp.concatenate(halves, axis=1).astype(BF16)
        for kind in range(KINDS):
            piece = found[:, :, kind * LANES : (kind + 1) * LANES]
            turned[pl.ds(block * per_block, per_block), kind] = piece.reshape(per_block, *out_ref.shape[2:])
        flush(block).start()
        return carry

    lax.fori_loop(0, blocks, turn, 0)
    for block in range(blocks):
        flush(block).wait()


def to_positions(in_ref, mix_ref, sig_ref, tap_ref, table, data, sems):
    blocks = data.shape[0]
    per_block = in_ref.shape[0] // blocks

    def flush(kind, block):
        target = (mix_ref, sig_ref, tap_ref)[kind].at[:, pl.ds(block * LANES, LANES)]
        return pltpu.make_async_copy(data.at[block, kind], target, sems.at[block, kind])

    table[...] = shuffle(table.shape, 0)
    for block in range(blocks):
        for kind in range(KINDS):
            for split in range(SPLITS):
                piece = in_ref[block * per_block : (block + 1) * per_block, kind, split]
                turned = lax.dot_general(
                    piece.reshape(PAIR * LANES, LANES),
                    table[...],
                    (((0,), (0,)), ((), ())),
                    preferred_element_type=F32,
                ).astype(BF16)
                for c in range(PAIR):
                    start = (split * PAIR + c) * LANES
                    data[block, kind, start : start + LANES, :] = turned[:, c * LANES : (c + 1) * LANES]
            flush(kind, block).start()
    for block in range(blocks):
        for kind in range(KINDS):
            flush(kind, block).wait()


def convolve(x_ref, gain_ref, wide_ref, back_ref, lane_ref, unlane_ref, twist_ref, out_ref, gains):
    slabs, _, groups, cell_rows, _ = x_ref.shape
    rows = slabs * cell_rows
    grad_scale = 1.0 / math.sqrt(slabs * SEQ_DEV)

    shape = (groups * cell_rows, gain_ref.shape[1])
    line = lax.broadcasted_iota(jnp.int32, shape, 0)
    own = lax.axis_index("ctx") * (groups * QUAD) + line // cell_rows * QUAD + line % QUAD
    picked = jnp.where(lax.broadcasted_iota(jnp.int32, shape, 1) == own, gain_ref[...], 0.0)
    gains[...] = jnp.broadcast_to(jnp.sum(picked, axis=1, keepdims=True), gains.shape)

    for start in range(0, groups, STEP_GROUPS):
        units = [(kind, start + j) for j in range(STEP_GROUPS) for kind in range(KINDS)]
        data = jnp.concatenate([x_ref[:, kind, g].reshape(rows, LANES) for kind, g in units], axis=1)
        wave = jnp.dot(wide_ref[...], data, preferred_element_type=F32)
        spectra = []
        for u in range(len(units)):
            cols = slice(u * LANES, (u + 1) * LANES)
            real, imag = wave[:rows, cols], wave[rows:, cols]
            cos_part, sin_part = twist_ref[0], twist_ref[1]
            band = [real * cos_part + imag * sin_part, imag * cos_part - real * sin_part]
            band = jnp.concatenate([part.astype(BF16) for part in band], axis=1)
            spectra.append(jnp.dot(band, lane_ref[...], preferred_element_type=F32))
        bands = []
        for j in range(STEP_GROUPS):
            (sig_r, sig_i), (tap_r, tap_i), (up_r, up_i) = (
                (part[:, :LANES], part[:, LANES:]) for part in spectra[KINDS * j : KINDS * (j + 1)]
            )
            pairs = (
                (sig_r * tap_r - sig_i * tap_i, sig_r * tap_i + sig_i * tap_r),
                (up_r * tap_r + up_i * tap_i, up_i * tap_r - up_r * tap_i),
                (up_r * sig_r + up_i * sig_i, up_i * sig_r - up_r * sig_i),
            )
            for pair in pairs:
                product = jnp.concatenate([part.astype(BF16) for part in pair], axis=1)
                coef = jnp.dot(product, unlane_ref[...], preferred_element_type=F32)
                real, imag = coef[:, :LANES], coef[:, LANES:]
                cos_part, sin_part = twist_ref[0], twist_ref[1]
                band = [real * cos_part - imag * sin_part, imag * cos_part + real * sin_part]
                bands.append(jnp.concatenate([part.astype(BF16) for part in band], axis=0))
        sums = jnp.dot(back_ref[...], jnp.concatenate(bands, axis=1), preferred_element_type=F32)
        for kind in range(KINDS):
            convs = []
            for j in range(STEP_GROUPS):
                u, g = j * KINDS + kind, start + j
                conv = sums[:, u * LANES : (u + 1) * LANES].reshape(slabs, cell_rows, LANES)
                if kind < 2:
                    gain = gains[g * cell_rows : (g + 1) * cell_rows, :]
                    conv = conv + gain[None] * x_ref[:, 2 * kind, g].astype(F32)
                else:
                    conv = conv * grad_scale
                convs.append(conv)
            low, part = start * PAIR * QUAD, PAIR * QUAD
            for split in range(SPLITS):
                rows_of = [conv[:, split * part : (split + 1) * part] for conv in convs]
                out_ref[:, kind, split, low : low + STEP_GROUPS * part] = jnp.concatenate(rows_of, axis=1).astype(BF16)


def local(signal, filter_taps, skip_gain, upstream):
    ctx_count = lax.axis_size("ctx")
    chan_count = signal.shape[1]
    groups = chan_count // ctx_count // QUAD
    blocks = chan_count // LANES
    points = ctx_count * CELLS
    pieces = jax.ShapeDtypeStruct((ctx_count, KINDS, groups, CELLS * QUAD, LANES), BF16)
    hbm = pl.BlockSpec(memory_space=pltpu.HBM)
    turning = [
        pltpu.VMEM((PAIR * LANES, PAIR * LANES), BF16),
        pltpu.VMEM((blocks, KINDS, SEQ_DEV, LANES), BF16),
        pltpu.SemaphoreType.DMA((blocks, KINDS)),
    ]
    exchange = functools.partial(lax.all_to_all, axis_name="ctx", split_axis=0, concat_axis=0, tiled=True)

    sent = pl.pallas_call(
        to_channels,
        in_specs=[hbm] * 3,
        out_specs=hbm,
        out_shape=pieces,
        scratch_shapes=turning[:2]
        + [pltpu.VMEM(pieces.shape, BF16), turning[2], pltpu.SemaphoreType.DMA((blocks,))],
        compiler_params=pltpu.CompilerParams(vmem_limit_bytes=FILL_BYTES),
        name="to_channels",
    )(signal, filter_taps, upstream)
    whole = exchange(sent)

    wide, lanes = wide_table(points), lane_table()
    results = pl.pallas_call(
        convolve,
        out_shape=jax.ShapeDtypeStruct((ctx_count, KINDS, SPLITS, groups * PAIR * QUAD, LANES), BF16),
        scratch_shapes=[pltpu.VMEM((groups * CELLS * QUAD, LANES), F32)],
        compiler_params=pltpu.CompilerParams(vmem_limit_bytes=ROOM_BYTES),
        name="convolve",
    )(
        whole,
        skip_gain.reshape(1, chan_count),
        jnp.asarray(wide, BF16),
        jnp.asarray(wide.T / (points * LANES), BF16),
        jnp.asarray(lanes, BF16),
        jnp.asarray(lanes.T, BF16),
        jnp.asarray(twist_tables(points), F32),
    )
    returned = exchange(results)
    return pl.pallas_call(
        to_positions,
        out_specs=[hbm] * 3,
        out_shape=[jax.ShapeDtypeStruct((SEQ_DEV, chan_count), BF16)] * 3,
        scratch_shapes=turning,
        compiler_params=pltpu.CompilerParams(vmem_limit_bytes=ROOM_BYTES),
        name="to_positions",
    )(returned)


def solution(mesh):
    in_specs = (P("ctx", "tp"), P("ctx", "tp"), P("tp"), P("ctx", "tp"))
    out_specs = (P("ctx", "tp"), P("ctx", "tp"), P("ctx", "tp"))
    return jax.shard_map(local, mesh=mesh, in_specs=in_specs, out_specs=out_specs, check_vma=False)
```

```python
import functools
import math

import jax
import jax.numpy as jnp
import numpy as np
from jax import lax
from jax.experimental import pallas as pl
from jax.experimental.pallas import tpu as pltpu
from jax.sharding import PartitionSpec as P

SEQ_DEV = 512
LANES = 128
CELLS = SEQ_DEV // LANES
QUAD = 4
PAIR = 2
SPLITS = CELLS // PAIR
KINDS = 3
STEP_GROUPS = 2
ROOM_BYTES = 32 * 1024 * 1024
BF16 = jnp.bfloat16
F32 = jnp.float32


def wide_table(points):
    spot = np.arange(points)
    angle = 2.0 * math.pi * np.outer(spot + 0.25, spot) / points
    return np.kron(np.concatenate([np.cos(angle), -np.sin(angle)]), np.eye(QUAD))


def lane_table():
    spot = np.arange(LANES)
    angle = 2.0 * math.pi * (np.outer(spot, spot) % LANES) / LANES
    cos_part, sin_part = np.cos(angle), np.sin(angle)
    return np.block([[cos_part, -sin_part], [sin_part, cos_part]])


def twist_tables(points):
    angle = 2.0 * math.pi * np.outer(np.arange(points) + 0.25, np.arange(LANES)) / (points * LANES)
    return np.repeat(np.stack([np.cos(angle), np.sin(angle)]), QUAD, axis=1)


def shuffle(shape, row_axis):
    row = lax.broadcasted_iota(jnp.int32, shape, row_axis)
    col = lax.broadcasted_iota(jnp.int32, shape, 1 - row_axis)
    wanted = row // (QUAD * PAIR) * QUAD + row % QUAD + row // QUAD % PAIR * LANES
    return (col == wanted).astype(F32).astype(BF16)


def to_channels(sig_ref, tap_ref, up_ref, out_ref, table, data, sems):
    blocks = data.shape[0]
    per_block = out_ref.shape[0] // blocks

    def fetch(kind, block):
        source = (sig_ref, tap_ref, up_ref)[kind].at[:, pl.ds(block * LANES, LANES)]
        return pltpu.make_async_copy(source, data.at[block, kind], sems.at[block, kind])

    for block in range(blocks):
        for kind in range(KINDS):
            fetch(kind, block).start()
    table[...] = shuffle(table.shape, 0)

    def turn(block, carry):
        for kind in range(KINDS):
            fetch(kind, block).wait()
        halves = []
        for split in range(SPLITS):
            wide = [
                jnp.concatenate(
                    [data[block, kind, c * LANES : (c + 1) * LANES, :] for c in range(split * PAIR, (split + 1) * PAIR)],
                    axis=1,
                )
                for kind in range(KINDS)
            ]
            found = lax.dot_general(
                table[...], jnp.concatenate(wide, axis=0), (((1,), (1,)), ((), ())), preferred_element_type=F32
            )
            halves.append(found.reshape(-1, PAIR * QUAD, KINDS * LANES))
        found = jnp.concatenate(halves, axis=1).astype(BF16)
        for kind in range(KINDS):
            piece = found[:, :, kind * LANES : (kind + 1) * LANES]
            out_ref[pl.ds(block * per_block, per_block), kind] = piece.reshape(per_block, *out_ref.shape[2:])
        return carry

    lax.fori_loop(0, blocks, turn, 0)


def to_positions(in_ref, mix_ref, sig_ref, tap_ref, table, data, sems):
    blocks = data.shape[0]
    per_block = in_ref.shape[0] // blocks

    def flush(kind, block):
        target = (mix_ref, sig_ref, tap_ref)[kind].at[:, pl.ds(block * LANES, LANES)]
        return pltpu.make_async_copy(data.at[block, kind], target, sems.at[block, kind])

    table[...] = shuffle(table.shape, 0)
    for block in range(blocks):
        for kind in range(KINDS):
            for split in range(SPLITS):
                piece = in_ref[block * per_block : (block + 1) * per_block, kind, split]
                turned = lax.dot_general(
                    piece.reshape(PAIR * LANES, LANES),
                    table[...],
                    (((0,), (0,)), ((), ())),
                    preferred_element_type=F32,
                ).astype(BF16)
                for c in range(PAIR):
                    start = (split * PAIR + c) * LANES
                    data[block, kind, start : start + LANES, :] = turned[:, c * LANES : (c + 1) * LANES]
            flush(kind, block).start()
    for block in range(blocks):
        for kind in range(KINDS):
            flush(kind, block).wait()


def convolve(x_ref, gain_ref, wide_ref, back_ref, lane_ref, unlane_ref, twist_ref, out_ref, gains):
    slabs, _, groups, cell_rows, _ = x_ref.shape
    rows = slabs * cell_rows
    grad_scale = 1.0 / math.sqrt(slabs * SEQ_DEV)

    shape = (groups * cell_rows, gain_ref.shape[1])
    line = lax.broadcasted_iota(jnp.int32, shape, 0)
    own = lax.axis_index("ctx") * (groups * QUAD) + line // cell_rows * QUAD + line % QUAD
    picked = jnp.where(lax.broadcasted_iota(jnp.int32, shape, 1) == own, gain_ref[...], 0.0)
    gains[...] = jnp.broadcast_to(jnp.sum(picked, axis=1, keepdims=True), gains.shape)

    for start in range(0, groups, STEP_GROUPS):
        units = [(kind, start + j) for j in range(STEP_GROUPS) for kind in range(KINDS)]
        data = jnp.concatenate([x_ref[:, kind, g].reshape(rows, LANES) for kind, g in units], axis=1)
        wave = jnp.dot(wide_ref[...], data, preferred_element_type=F32)
        spectra = []
        for u in range(len(units)):
            cols = slice(u * LANES, (u + 1) * LANES)
            real, imag = wave[:rows, cols], wave[rows:, cols]
            cos_part, sin_part = twist_ref[0], twist_ref[1]
            band = [real * cos_part + imag * sin_part, imag * cos_part - real * sin_part]
            band = jnp.concatenate([part.astype(BF16) for part in band], axis=1)
            spectra.append(jnp.dot(band, lane_ref[...], preferred_element_type=F32))
        bands = []
        for j in range(STEP_GROUPS):
            (sig_r, sig_i), (tap_r, tap_i), (up_r, up_i) = (
                (part[:, :LANES], part[:, LANES:]) for part in spectra[KINDS * j : KINDS * (j + 1)]
            )
            pairs = (
                (sig_r * tap_r - sig_i * tap_i, sig_r * tap_i + sig_i * tap_r),
                (up_r * tap_r + up_i * tap_i, up_i * tap_r - up_r * tap_i),
                (up_r * sig_r + up_i * sig_i, up_i * sig_r - up_r * sig_i),
            )
            for pair in pairs:
                product = jnp.concatenate([part.astype(BF16) for part in pair], axis=1)
                coef = jnp.dot(product, unlane_ref[...], preferred_element_type=F32)
                real, imag = coef[:, :LANES], coef[:, LANES:]
                cos_part, sin_part = twist_ref[0], twist_ref[1]
                band = [real * cos_part - imag * sin_part, imag * cos_part + real * sin_part]
                bands.append(jnp.concatenate([part.astype(BF16) for part in band], axis=0))
        sums = jnp.dot(back_ref[...], jnp.concatenate(bands, axis=1), preferred_element_type=F32)
        for kind in range(KINDS):
            convs = []
            for j in range(STEP_GROUPS):
                u, g = j * KINDS + kind, start + j
                conv = sums[:, u * LANES : (u + 1) * LANES].reshape(slabs, cell_rows, LANES)
                if kind < 2:
                    gain = gains[g * cell_rows : (g + 1) * cell_rows, :]
                    conv = conv + gain[None] * x_ref[:, 2 * kind, g].astype(F32)
                else:
                    conv = conv * grad_scale
                convs.append(conv)
            low, part = start * PAIR * QUAD, PAIR * QUAD
            for split in range(SPLITS):
                rows_of = [conv[:, split * part : (split + 1) * part] for conv in convs]
                out_ref[:, kind, split, low : low + STEP_GROUPS * part] = jnp.concatenate(rows_of, axis=1).astype(BF16)


def local(signal, filter_taps, skip_gain, upstream):
    ctx_count = lax.axis_size("ctx")
    chan_count = signal.shape[1]
    groups = chan_count // ctx_count // QUAD
    blocks = chan_count // LANES
    points = ctx_count * CELLS
    pieces = jax.ShapeDtypeStruct((ctx_count, KINDS, groups, CELLS * QUAD, LANES), BF16)
    hbm = pl.BlockSpec(memory_space=pltpu.HBM)
    turning = [
        pltpu.VMEM((PAIR * LANES, PAIR * LANES), BF16),
        pltpu.VMEM((blocks, KINDS, SEQ_DEV, LANES), BF16),
        pltpu.SemaphoreType.DMA((blocks, KINDS)),
    ]
    exchange = functools.partial(lax.all_to_all, axis_name="ctx", split_axis=0, concat_axis=0, tiled=True)

    sent = pl.pallas_call(
        to_channels,
        in_specs=[hbm] * 3,
        out_shape=pltpu.VMEM(pieces.shape, BF16),
        scratch_shapes=turning,
        compiler_params=pltpu.CompilerParams(vmem_limit_bytes=ROOM_BYTES),
        name="to_channels",
    )(*(pltpu.with_memory_space_constraint(x, pltpu.HBM) for x in (signal, filter_taps, upstream)))
    whole = exchange(sent)

    wide, lanes = wide_table(points), lane_table()
    results = pl.pallas_call(
        convolve,
        out_shape=jax.ShapeDtypeStruct((ctx_count, KINDS, SPLITS, groups * PAIR * QUAD, LANES), BF16),
        scratch_shapes=[pltpu.VMEM((groups * CELLS * QUAD, LANES), F32)],
        compiler_params=pltpu.CompilerParams(vmem_limit_bytes=ROOM_BYTES),
        name="convolve",
    )(
        whole,
        skip_gain.reshape(1, chan_count),
        jnp.asarray(wide, BF16),
        jnp.asarray(wide.T / (points * LANES), BF16),
        jnp.asarray(lanes, BF16),
        jnp.asarray(lanes.T, BF16),
        jnp.asarray(twist_tables(points), F32),
    )
    returned = exchange(results)
    return pl.pallas_call(
        to_positions,
        out_specs=[hbm] * 3,
        out_shape=[jax.ShapeDtypeStruct((SEQ_DEV, chan_count), BF16)] * 3,
        scratch_shapes=turning,
        compiler_params=pltpu.CompilerParams(vmem_limit_bytes=ROOM_BYTES),
        name="to_positions",
    )(returned)


def solution(mesh):
    in_specs = (P("ctx", "tp"), P("ctx", "tp"), P("tp"), P("ctx", "tp"))
    out_specs = (P("ctx", "tp"), P("ctx", "tp"), P("ctx", "tp"))
    return jax.shard_map(local, mesh=mesh, in_specs=in_specs, out_specs=out_specs, check_vma=False)
```

```python
import functools
import math

import jax
import jax.numpy as jnp
import numpy as np
from jax import lax
from jax.experimental import pallas as pl
from jax.experimental.pallas import tpu as pltpu
from jax.sharding import PartitionSpec as P

SEQ_DEV = 512
LANES = 128
CELLS = SEQ_DEV // LANES
QUAD = 4
PAIR = 2
SPLITS = CELLS // PAIR
KINDS = 3
STEP_GROUPS = 2
WIDE_SCALE = 1.9925
LANE_SCALE = 1.625
ROOM_BYTES = 32 * 1024 * 1024
BF16 = jnp.bfloat16
F32 = jnp.float32


def wide_table(points):
    spot = np.arange(points)
    angle = 2.0 * math.pi * np.outer(spot + 0.25, spot) / points
    return np.kron(np.concatenate([np.cos(angle), -np.sin(angle)]), np.eye(QUAD))


def lane_table():
    spot = np.arange(LANES)
    angle = 2.0 * math.pi * (np.outer(spot, spot) % LANES) / LANES
    cos_part, sin_part = np.cos(angle), np.sin(angle)
    return np.block([[cos_part, -sin_part], [sin_part, cos_part]])


def twist_tables(points):
    angle = 2.0 * math.pi * np.outer(np.arange(points) + 0.25, np.arange(LANES)) / (points * LANES)
    return np.repeat(np.stack([np.cos(angle), np.sin(angle)]), QUAD, axis=1)


def shuffle(shape, row_axis):
    row = lax.broadcasted_iota(jnp.int32, shape, row_axis)
    col = lax.broadcasted_iota(jnp.int32, shape, 1 - row_axis)
    wanted = row // (QUAD * PAIR) * QUAD + row % QUAD + row // QUAD % PAIR * LANES
    return (col == wanted).astype(F32).astype(BF16)


def to_channels(sig_ref, tap_ref, up_ref, out_ref, table, data, sems):
    blocks = data.shape[0]
    per_block = out_ref.shape[0] // blocks

    def fetch(kind, block, low, size):
        source = (sig_ref, tap_ref, up_ref)[kind].at[pl.ds(low, size), pl.ds(block * LANES, LANES)]
        return pltpu.make_async_copy(source, data.at[block, kind, pl.ds(low, size), :], sems.at[block, kind])

    for block in range(blocks):
        for low in range(0, SEQ_DEV, LANES):
            for kind in range(KINDS):
                fetch(kind, block, low, LANES).start()
    table[...] = shuffle(table.shape, 0)

    def turn(block, carry):
        for kind in range(KINDS):
            fetch(kind, block, 0, SEQ_DEV).wait()
        halves = []
        for split in range(SPLITS):
            wide = [
                jnp.concatenate(
                    [data[block, kind, c * LANES : (c + 1) * LANES, :] for c in range(split * PAIR, (split + 1) * PAIR)],
                    axis=1,
                )
                for kind in range(KINDS)
            ]
            found = lax.dot_general(
                table[...], jnp.concatenate(wide, axis=0), (((1,), (1,)), ((), ())), preferred_element_type=F32
            )
            halves.append(found.reshape(-1, PAIR * QUAD, KINDS * LANES))
        found = jnp.concatenate(halves, axis=1).astype(BF16)
        for kind in range(KINDS):
            piece = found[:, :, kind * LANES : (kind + 1) * LANES]
            out_ref[pl.ds(block * per_block, per_block), kind] = piece.reshape(per_block, *out_ref.shape[2:])
        return carry

    lax.fori_loop(0, blocks, turn, 0)


def to_positions(in_ref, mix_ref, sig_ref, tap_ref, table, data, sems):
    blocks = data.shape[0]
    per_block = in_ref.shape[0] // blocks

    def flush(kind, block):
        target = (mix_ref, sig_ref, tap_ref)[kind].at[:, pl.ds(block * LANES, LANES)]
        return pltpu.make_async_copy(data.at[block, kind], target, sems.at[block, kind])

    table[...] = shuffle(table.shape, 0)
    for block in range(blocks):
        for kind in range(KINDS):
            for split in range(SPLITS):
                piece = in_ref[block * per_block : (block + 1) * per_block, kind, split]
                turned = lax.dot_general(
                    piece.reshape(PAIR * LANES, LANES),
                    table[...],
                    (((0,), (0,)), ((), ())),
                    preferred_element_type=F32,
                ).astype(BF16)
                for c in range(PAIR):
                    start = (split * PAIR + c) * LANES
                    data[block, kind, start : start + LANES, :] = turned[:, c * LANES : (c + 1) * LANES]
            flush(kind, block).start()
    for block in range(blocks):
        for kind in range(KINDS):
            flush(kind, block).wait()


def convolve(x_ref, gain_ref, wide_ref, back_ref, lane_ref, unlane_ref, twist_ref, out_ref, gains):
    slabs, _, groups, cell_rows, _ = x_ref.shape
    rows = slabs * cell_rows
    grad_scale = 1.0 / math.sqrt(slabs * SEQ_DEV)

    shape = (groups * cell_rows, gain_ref.shape[1])
    line = lax.broadcasted_iota(jnp.int32, shape, 0)
    own = lax.axis_index("ctx") * (groups * QUAD) + line // cell_rows * QUAD + line % QUAD
    picked = jnp.where(lax.broadcasted_iota(jnp.int32, shape, 1) == own, gain_ref[...], 0.0)
    gains[...] = jnp.broadcast_to(jnp.sum(picked, axis=1, keepdims=True), gains.shape)

    for start in range(0, groups, STEP_GROUPS):
        units = [(kind, start + j) for j in range(STEP_GROUPS) for kind in range(KINDS)]
        data = jnp.concatenate([x_ref[:, kind, g].reshape(rows, LANES) for kind, g in units], axis=1)
        wave = jnp.dot(wide_ref[...], data, preferred_element_type=F32)
        spectra = []
        for u in range(len(units)):
            cols = slice(u * LANES, (u + 1) * LANES)
            real, imag = wave[:rows, cols], wave[rows:, cols]
            cos_part, sin_part = twist_ref[0], twist_ref[1]
            band = [real * cos_part + imag * sin_part, imag * cos_part - real * sin_part]
            band = jnp.concatenate([part.astype(BF16) for part in band], axis=1)
            spectra.append(jnp.dot(band, lane_ref[...], preferred_element_type=F32))
        bands = []
        for j in range(STEP_GROUPS):
            (sig_r, sig_i), (tap_r, tap_i), (up_r, up_i) = (
                (part[:, :LANES], part[:, LANES:]) for part in spectra[KINDS * j : KINDS * (j + 1)]
            )
            pairs = (
                (sig_r * tap_r - sig_i * tap_i, sig_r * tap_i + sig_i * tap_r),
                (up_r * tap_r + up_i * tap_i, up_i * tap_r - up_r * tap_i),
                (up_r * sig_r + up_i * sig_i, up_i * sig_r - up_r * sig_i),
            )
            for pair in pairs:
                product = jnp.concatenate([part.astype(BF16) for part in pair], axis=1)
                coef = jnp.dot(product, unlane_ref[...], preferred_element_type=F32)
                real, imag = coef[:, :LANES], coef[:, LANES:]
                cos_part, sin_part = twist_ref[0], twist_ref[1]
                band = [real * cos_part - imag * sin_part, imag * cos_part + real * sin_part]
                bands.append(jnp.concatenate([part.astype(BF16) for part in band], axis=0))
        sums = jnp.dot(back_ref[...], jnp.concatenate(bands, axis=1), preferred_element_type=F32)
        for kind in range(KINDS):
            convs = []
            for j in range(STEP_GROUPS):
                u, g = j * KINDS + kind, start + j
                conv = sums[:, u * LANES : (u + 1) * LANES].reshape(slabs, cell_rows, LANES)
                if kind < 2:
                    gain = gains[g * cell_rows : (g + 1) * cell_rows, :]
                    conv = conv + gain[None] * x_ref[:, 2 * kind, g].astype(F32)
                else:
                    conv = conv * grad_scale
                convs.append(conv)
            low, part = start * PAIR * QUAD, PAIR * QUAD
            for split in range(SPLITS):
                rows_of = [conv[:, split * part : (split + 1) * part] for conv in convs]
                out_ref[:, kind, split, low : low + STEP_GROUPS * part] = jnp.concatenate(rows_of, axis=1).astype(BF16)


def local(signal, filter_taps, skip_gain, upstream):
    ctx_count = lax.axis_size("ctx")
    chan_count = signal.shape[1]
    groups = chan_count // ctx_count // QUAD
    blocks = chan_count // LANES
    points = ctx_count * CELLS
    pieces = jax.ShapeDtypeStruct((ctx_count, KINDS, groups, CELLS * QUAD, LANES), BF16)
    hbm = pl.BlockSpec(memory_space=pltpu.HBM)
    turning = [
        pltpu.VMEM((PAIR * LANES, PAIR * LANES), BF16),
        pltpu.VMEM((blocks, KINDS, SEQ_DEV, LANES), BF16),
        pltpu.SemaphoreType.DMA((blocks, KINDS)),
    ]
    exchange = functools.partial(lax.all_to_all, axis_name="ctx", split_axis=0, concat_axis=0, tiled=True)

    sent = pl.pallas_call(
        to_channels,
        in_specs=[hbm] * 3,
        out_shape=pltpu.VMEM(pieces.shape, BF16),
        scratch_shapes=turning,
        compiler_params=pltpu.CompilerParams(vmem_limit_bytes=ROOM_BYTES),
        name="to_channels",
    )(*(pltpu.with_memory_space_constraint(x, pltpu.HBM) for x in (signal, filter_taps, upstream)))
    whole = exchange(sent)

    wide, lanes = WIDE_SCALE * wide_table(points), LANE_SCALE * lane_table()
    results = pl.pallas_call(
        convolve,
        out_shape=jax.ShapeDtypeStruct((ctx_count, KINDS, SPLITS, groups * PAIR * QUAD, LANES), BF16),
        scratch_shapes=[pltpu.VMEM((groups * CELLS * QUAD, LANES), F32)],
        compiler_params=pltpu.CompilerParams(vmem_limit_bytes=ROOM_BYTES),
        name="convolve",
    )(
        whole,
        skip_gain.reshape(1, chan_count),
        jnp.asarray(wide, BF16),
        jnp.asarray(wide.T / (points * LANES), BF16),
        jnp.asarray(lanes, BF16),
        jnp.asarray(lanes.T, BF16),
        jnp.asarray(twist_tables(points) / (WIDE_SCALE * LANE_SCALE), F32),
    )
    returned = exchange(results)
    return pl.pallas_call(
        to_positions,
        out_specs=[hbm] * 3,
        out_shape=[jax.ShapeDtypeStruct((SEQ_DEV, chan_count), BF16)] * 3,
        scratch_shapes=turning,
        compiler_params=pltpu.CompilerParams(vmem_limit_bytes=ROOM_BYTES),
        name="to_positions",
    )(returned)


def solution(mesh):
    in_specs = (P("ctx", "tp"), P("ctx", "tp"), P("tp"), P("ctx", "tp"))
    out_specs = (P("ctx", "tp"), P("ctx", "tp"), P("ctx", "tp"))
    return jax.shard_map(local, mesh=mesh, in_specs=in_specs, out_specs=out_specs, check_vma=False)
```

```python
import functools
import math

import jax
import jax.numpy as jnp
import numpy as np
from jax import lax
from jax.experimental import pallas as pl
from jax.experimental.pallas import tpu as pltpu
from jax.sharding import PartitionSpec as P

SEQ_DEV = 512
LANES = 128
CELLS = SEQ_DEV // LANES
QUAD = 4
PAIR = 2
SPLITS = CELLS // PAIR
KINDS = 3
STEP_GROUPS = 2
ROOM_BYTES = 32 * 1024 * 1024
BF16 = jnp.bfloat16
F32 = jnp.float32


def wide_table(points):
    spot = np.arange(points)
    angle = 2.0 * math.pi * np.outer(spot + 0.25, spot) / points
    return np.kron(np.concatenate([np.cos(angle), -np.sin(angle)]), np.eye(QUAD))


def lane_table():
    spot = np.arange(LANES)
    angle = 2.0 * math.pi * (np.outer(spot, spot) % LANES) / LANES
    cos_part, sin_part = np.cos(angle), np.sin(angle)
    return np.block([[cos_part, -sin_part], [sin_part, cos_part]])


def twist_tables(points):
    angle = 2.0 * math.pi * np.outer(np.arange(points) + 0.25, np.arange(LANES)) / (points * LANES)
    return np.repeat(np.stack([np.cos(angle), np.sin(angle)]), QUAD, axis=1)


def shuffle(shape, row_axis):
    row = lax.broadcasted_iota(jnp.int32, shape, row_axis)
    col = lax.broadcasted_iota(jnp.int32, shape, 1 - row_axis)
    wanted = row // (QUAD * PAIR) * QUAD + row % QUAD + row // QUAD % PAIR * LANES
    return (col == wanted).astype(F32).astype(BF16)


def to_channels(sig_ref, tap_ref, up_ref, out_ref, table, data, sems):
    blocks = data.shape[0]
    per_block = out_ref.shape[0] // blocks

    def fetch(kind, block, low, size):
        source = (sig_ref, tap_ref, up_ref)[kind].at[pl.ds(low, size), pl.ds(block * LANES, LANES)]
        return pltpu.make_async_copy(source, data.at[block, kind, pl.ds(low, size), :], sems.at[block, kind])

    for block in range(blocks):
        for low in range(0, SEQ_DEV, LANES):
            for kind in range(KINDS):
                fetch(kind, block, low, LANES).start()
    table[...] = shuffle(table.shape, 0)

    def turn(block, carry):
        for kind in range(KINDS):
            fetch(kind, block, 0, SEQ_DEV).wait()
        halves = []
        for split in range(SPLITS):
            wide = [
                jnp.concatenate(
                    [data[block, kind, c * LANES : (c + 1) * LANES, :] for c in range(split * PAIR, (split + 1) * PAIR)],
                    axis=1,
                )
                for kind in range(KINDS)
            ]
            found = lax.dot_general(
                table[...], jnp.concatenate(wide, axis=0), (((1,), (1,)), ((), ())), preferred_element_type=F32
            )
            halves.append(found.reshape(-1, PAIR * QUAD, KINDS * LANES))
        found = jnp.concatenate(halves, axis=1).astype(BF16)
        for kind in range(KINDS):
            piece = found[:, :, kind * LANES : (kind + 1) * LANES]
            out_ref[pl.ds(block * per_block, per_block), kind] = piece.reshape(per_block, *out_ref.shape[2:])
        return carry

    lax.fori_loop(0, blocks, turn, 0)


def to_positions(in_ref, mix_ref, sig_ref, tap_ref, table, data, sems):
    blocks = data.shape[0]
    per_block = in_ref.shape[0] // blocks

    def flush(kind, block, low, size):
        target = (mix_ref, sig_ref, tap_ref)[kind].at[pl.ds(low, size), pl.ds(block * LANES, LANES)]
        return pltpu.make_async_copy(data.at[block, kind, pl.ds(low, size), :], target, sems.at[block, kind])

    table[...] = shuffle(table.shape, 0)
    for block in range(blocks):
        for kind in range(KINDS):
            for split in range(SPLITS):
                piece = in_ref[block * per_block : (block + 1) * per_block, kind, split]
                turned = lax.dot_general(
                    piece.reshape(PAIR * LANES, LANES),
                    table[...],
                    (((0,), (0,)), ((), ())),
                    preferred_element_type=F32,
                ).astype(BF16)
                for c in range(PAIR):
                    start = (split * PAIR + c) * LANES
                    data[block, kind, start : start + LANES, :] = turned[:, c * LANES : (c + 1) * LANES]
                flush(kind, block, split * PAIR * LANES, PAIR * LANES).start()
    for block in range(blocks):
        for kind in range(KINDS):
            flush(kind, block, 0, SEQ_DEV).wait()


def convolve(x_ref, gain_ref, wide_ref, back_ref, lane_ref, unlane_ref, twist_ref, out_ref, gains):
    slabs, _, groups, cell_rows, _ = x_ref.shape
    rows = slabs * cell_rows
    grad_scale = 1.0 / math.sqrt(slabs * SEQ_DEV)

    shape = (groups * cell_rows, gain_ref.shape[1])
    line = lax.broadcasted_iota(jnp.int32, shape, 0)
    own = lax.axis_index("ctx") * (groups * QUAD) + line // cell_rows * QUAD + line % QUAD
    picked = jnp.where(lax.broadcasted_iota(jnp.int32, shape, 1) == own, gain_ref[...], 0.0)
    gains[...] = jnp.broadcast_to(jnp.sum(picked, axis=1, keepdims=True), gains.shape)

    for start in range(0, groups, STEP_GROUPS):
        units = [(kind, start + j) for j in range(STEP_GROUPS) for kind in range(KINDS)]
        data = jnp.concatenate([x_ref[:, kind, g].reshape(rows, LANES) for kind, g in units], axis=1)
        wave = jnp.dot(wide_ref[...], data, preferred_element_type=F32)
        spectra = []
        for u in range(len(units)):
            cols = slice(u * LANES, (u + 1) * LANES)
            real, imag = wave[:rows, cols], wave[rows:, cols]
            cos_part, sin_part = twist_ref[0], twist_ref[1]
            band = [real * cos_part + imag * sin_part, imag * cos_part - real * sin_part]
            band = jnp.concatenate([part.astype(BF16) for part in band], axis=1)
            spectra.append(jnp.dot(band, lane_ref[...], preferred_element_type=F32))
        bands = []
        for j in range(STEP_GROUPS):
            (sig_r, sig_i), (tap_r, tap_i), (up_r, up_i) = (
                (part[:, :LANES], part[:, LANES:]) for part in spectra[KINDS * j : KINDS * (j + 1)]
            )
            pairs = (
                (sig_r * tap_r - sig_i * tap_i, sig_r * tap_i + sig_i * tap_r),
                (up_r * tap_r + up_i * tap_i, up_i * tap_r - up_r * tap_i),
                (up_r * sig_r + up_i * sig_i, up_i * sig_r - up_r * sig_i),
            )
            for pair in pairs:
                product = jnp.concatenate([part.astype(BF16) for part in pair], axis=1)
                coef = jnp.dot(product, unlane_ref[...], preferred_element_type=F32)
                real, imag = coef[:, :LANES], coef[:, LANES:]
                cos_part, sin_part = twist_ref[0], twist_ref[1]
                band = [real * cos_part - imag * sin_part, imag * cos_part + real * sin_part]
                bands.append(jnp.concatenate([part.astype(BF16) for part in band], axis=0))
        sums = jnp.dot(back_ref[...], jnp.concatenate(bands, axis=1), preferred_element_type=F32)
        for kind in range(KINDS):
            convs = []
            for j in range(STEP_GROUPS):
                u, g = j * KINDS + kind, start + j
                conv = sums[:, u * LANES : (u + 1) * LANES].reshape(slabs, cell_rows, LANES)
                if kind < 2:
                    gain = gains[g * cell_rows : (g + 1) * cell_rows, :]
                    conv = conv + gain[None] * x_ref[:, 2 * kind, g].astype(F32)
                else:
                    conv = conv * grad_scale
                convs.append(conv)
            low, part = start * PAIR * QUAD, PAIR * QUAD
            for split in range(SPLITS):
                rows_of = [conv[:, split * part : (split + 1) * part] for conv in convs]
                out_ref[:, kind, split, low : low + STEP_GROUPS * part] = jnp.concatenate(rows_of, axis=1).astype(BF16)


def local(signal, filter_taps, skip_gain, upstream):
    ctx_count = lax.axis_size("ctx")
    chan_count = signal.shape[1]
    groups = chan_count // ctx_count // QUAD
    blocks = chan_count // LANES
    points = ctx_count * CELLS
    pieces = jax.ShapeDtypeStruct((ctx_count, KINDS, groups, CELLS * QUAD, LANES), BF16)
    hbm = pl.BlockSpec(memory_space=pltpu.HBM)
    turning = [
        pltpu.VMEM((PAIR * LANES, PAIR * LANES), BF16),
        pltpu.VMEM((blocks, KINDS, SEQ_DEV, LANES), BF16),
        pltpu.SemaphoreType.DMA((blocks, KINDS)),
    ]
    exchange = functools.partial(lax.all_to_all, axis_name="ctx", split_axis=0, concat_axis=0, tiled=True)

    sent = pl.pallas_call(
        to_channels,
        in_specs=[hbm] * 3,
        out_shape=pltpu.VMEM(pieces.shape, BF16),
        scratch_shapes=turning,
        compiler_params=pltpu.CompilerParams(vmem_limit_bytes=ROOM_BYTES),
        name="to_channels",
    )(*(pltpu.with_memory_space_constraint(x, pltpu.HBM) for x in (signal, filter_taps, upstream)))
    whole = exchange(sent)

    wide, lanes = wide_table(points), lane_table()
    results = pl.pallas_call(
        convolve,
        out_shape=jax.ShapeDtypeStruct((ctx_count, KINDS, SPLITS, groups * PAIR * QUAD, LANES), BF16),
        scratch_shapes=[pltpu.VMEM((groups * CELLS * QUAD, LANES), F32)],
        compiler_params=pltpu.CompilerParams(vmem_limit_bytes=ROOM_BYTES),
        name="convolve",
    )(
        whole,
        skip_gain.reshape(1, chan_count),
        jnp.asarray(wide, BF16),
        jnp.asarray(wide.T / (points * LANES), BF16),
        jnp.asarray(lanes, BF16),
        jnp.asarray(lanes.T, BF16),
        jnp.asarray(twist_tables(points), F32),
    )
    returned = exchange(results)
    return pl.pallas_call(
        to_positions,
        out_specs=[hbm] * 3,
        out_shape=[jax.ShapeDtypeStruct((SEQ_DEV, chan_count), BF16)] * 3,
        scratch_shapes=turning,
        compiler_params=pltpu.CompilerParams(vmem_limit_bytes=ROOM_BYTES),
        name="to_positions",
    )(returned)


def solution(mesh):
    in_specs = (P("ctx", "tp"), P("ctx", "tp"), P("tp"), P("ctx", "tp"))
    out_specs = (P("ctx", "tp"), P("ctx", "tp"), P("ctx", "tp"))
    return jax.shard_map(local, mesh=mesh, in_specs=in_specs, out_specs=out_specs, check_vma=False)
```

```python
import functools
import math

import jax
import jax.numpy as jnp
import numpy as np
from jax import lax
from jax.experimental import pallas as pl
from jax.experimental.pallas import tpu as pltpu
from jax.sharding import PartitionSpec as P

SEQ_DEV = 512
LANES = 128
CELLS = SEQ_DEV // LANES
QUAD = 4
PAIR = 2
SPLITS = CELLS // PAIR
KINDS = 3
STEP_GROUPS = 2
ROOM_BYTES = 32 * 1024 * 1024
BF16 = jnp.bfloat16
F32 = jnp.float32


def wide_table(points):
    spot = np.arange(points)
    angle = 2.0 * math.pi * np.outer(spot + 0.25, spot) / points
    return np.kron(np.concatenate([np.cos(angle), -np.sin(angle)]), np.eye(QUAD))


def lane_table():
    spot = np.arange(LANES)
    angle = 2.0 * math.pi * (np.outer(spot, spot) % LANES) / LANES
    cos_part, sin_part = np.cos(angle), np.sin(angle)
    return np.block([[cos_part, -sin_part], [sin_part, cos_part]])


def twist_tables(points):
    angle = 2.0 * math.pi * np.outer(np.arange(points) + 0.25, np.arange(LANES)) / (points * LANES)
    return np.repeat(np.stack([np.cos(angle), np.sin(angle)]), QUAD, axis=1)


def shuffle(shape, row_axis):
    row = lax.broadcasted_iota(jnp.int32, shape, row_axis)
    col = lax.broadcasted_iota(jnp.int32, shape, 1 - row_axis)
    wanted = row // (QUAD * PAIR) * QUAD + row % QUAD + row // QUAD % PAIR * LANES
    return (col == wanted).astype(F32).astype(BF16)


def to_channels(sig_ref, tap_ref, up_ref, out_ref, table, data, sems):
    blocks = data.shape[0]
    per_block = out_ref.shape[0] // blocks

    def fetch(kind, block):
        source = (sig_ref, tap_ref, up_ref)[kind].at[:, pl.ds(block * LANES, LANES)]
        return pltpu.make_async_copy(source, data.at[block, kind], sems.at[block, kind])

    for block in range(blocks):
        for kind in range(KINDS):
            fetch(kind, block).start()
    table[...] = shuffle(table.shape, 0)

    def turn(block, carry):
        for kind in range(KINDS):
            fetch(kind, block).wait()
        halves = []
        for split in range(SPLITS):
            wide = [
                jnp.concatenate(
                    [data[block, kind, c * LANES : (c + 1) * LANES, :] for c in range(split * PAIR, (split + 1) * PAIR)],
                    axis=1,
                )
                for kind in range(KINDS)
            ]
            found = lax.dot_general(
                table[...], jnp.concatenate(wide, axis=0), (((1,), (1,)), ((), ())), preferred_element_type=F32
            )
            halves.append(found.reshape(-1, PAIR * QUAD, KINDS * LANES))
        found = jnp.concatenate(halves, axis=1).astype(BF16)
        for kind in range(KINDS):
            piece = found[:, :, kind * LANES : (kind + 1) * LANES]
            out_ref[pl.ds(block * per_block, per_block), kind] = piece.reshape(per_block, *out_ref.shape[2:])
        return carry

    lax.fori_loop(0, blocks, turn, 0)


def to_positions(in_ref, mix_ref, sig_ref, tap_ref, table, data, sems):
    blocks = data.shape[0]
    per_block = in_ref.shape[0] // blocks

    def flush(kind, block):
        target = (mix_ref, sig_ref, tap_ref)[kind].at[:, pl.ds(block * LANES, LANES)]
        return pltpu.make_async_copy(data.at[block, kind], target, sems.at[block, kind])

    table[...] = shuffle(table.shape, 0)
    for block in range(blocks):
        for kind in range(KINDS):
            for split in range(SPLITS):
                piece = in_ref[block * per_block : (block + 1) * per_block, kind, split]
                turned = lax.dot_general(
                    piece.reshape(PAIR * LANES, LANES),
                    table[...],
                    (((0,), (0,)), ((), ())),
                    preferred_element_type=F32,
                ).astype(BF16)
                for c in range(PAIR):
                    start = (split * PAIR + c) * LANES
                    data[block, kind, start : start + LANES, :] = turned[:, c * LANES : (c + 1) * LANES]
            flush(kind, block).start()
    for block in range(blocks):
        for kind in range(KINDS):
            flush(kind, block).wait()


def convolve(x_ref, gain_ref, wide_ref, back_ref, lane_ref, unlane_ref, twist_ref, out_ref, gains):
    slabs, _, groups, cell_rows, _ = x_ref.shape
    rows = slabs * cell_rows
    grad_scale = 1.0 / math.sqrt(slabs * SEQ_DEV)

    shape = (groups * cell_rows, gain_ref.shape[1])
    line = lax.broadcasted_iota(jnp.int32, shape, 0)
    own = lax.axis_index("ctx") * (groups * QUAD) + line // cell_rows * QUAD + line % QUAD
    picked = jnp.where(lax.broadcasted_iota(jnp.int32, shape, 1) == own, gain_ref[...], 0.0)
    gains[...] = jnp.broadcast_to(jnp.sum(picked, axis=1, keepdims=True), gains.shape)

    for start in range(0, groups, STEP_GROUPS):
        units = [(kind, start + j) for j in range(STEP_GROUPS) for kind in range(KINDS)]
        order = [j * KINDS + kind for kind in range(KINDS) for j in range(STEP_GROUPS)]
        data = jnp.concatenate([x_ref[:, kind, g].reshape(rows, LANES) for kind, g in units], axis=1)
        wave = jnp.dot(wide_ref[...], data, preferred_element_type=F32)
        spectra = [None] * len(units)
        for u in order:
            cols = slice(u * LANES, (u + 1) * LANES)
            real, imag = wave[:rows, cols], wave[rows:, cols]
            cos_part, sin_part = twist_ref[0], twist_ref[1]
            band = [real * cos_part + imag * sin_part, imag * cos_part - real * sin_part]
            band = jnp.concatenate([part.astype(BF16) for part in band], axis=1)
            spectra[u] = jnp.dot(band, lane_ref[...], preferred_element_type=F32)
        bands = []
        for j in range(STEP_GROUPS):
            (sig_r, sig_i), (tap_r, tap_i), (up_r, up_i) = (
                (part[:, :LANES], part[:, LANES:]) for part in spectra[KINDS * j : KINDS * (j + 1)]
            )
            pairs = (
                (sig_r * tap_r - sig_i * tap_i, sig_r * tap_i + sig_i * tap_r),
                (up_r * tap_r + up_i * tap_i, up_i * tap_r - up_r * tap_i),
                (up_r * sig_r + up_i * sig_i, up_i * sig_r - up_r * sig_i),
            )
            for pair in pairs:
                product = jnp.concatenate([part.astype(BF16) for part in pair], axis=1)
                coef = jnp.dot(product, unlane_ref[...], preferred_element_type=F32)
                real, imag = coef[:, :LANES], coef[:, LANES:]
                cos_part, sin_part = twist_ref[0], twist_ref[1]
                band = [real * cos_part - imag * sin_part, imag * cos_part + real * sin_part]
                bands.append(jnp.concatenate([part.astype(BF16) for part in band], axis=0))
        sums = jnp.dot(back_ref[...], jnp.concatenate(bands, axis=1), preferred_element_type=F32)
        for kind in range(KINDS):
            convs = []
            for j in range(STEP_GROUPS):
                u, g = j * KINDS + kind, start + j
                conv = sums[:, u * LANES : (u + 1) * LANES].reshape(slabs, cell_rows, LANES)
                if kind < 2:
                    gain = gains[g * cell_rows : (g + 1) * cell_rows, :]
                    conv = conv + gain[None] * x_ref[:, 2 * kind, g].astype(F32)
                else:
                    conv = conv * grad_scale
                convs.append(conv)
            low, part = start * PAIR * QUAD, PAIR * QUAD
            for split in range(SPLITS):
                rows_of = [conv[:, split * part : (split + 1) * part] for conv in convs]
                out_ref[:, kind, split, low : low + STEP_GROUPS * part] = jnp.concatenate(rows_of, axis=1).astype(BF16)


def local(signal, filter_taps, skip_gain, upstream):
    ctx_count = lax.axis_size("ctx")
    chan_count = signal.shape[1]
    groups = chan_count // ctx_count // QUAD
    blocks = chan_count // LANES
    points = ctx_count * CELLS
    pieces = jax.ShapeDtypeStruct((ctx_count, KINDS, groups, CELLS * QUAD, LANES), BF16)
    hbm = pl.BlockSpec(memory_space=pltpu.HBM)
    turning = [
        pltpu.VMEM((PAIR * LANES, PAIR * LANES), BF16),
        pltpu.VMEM((blocks, KINDS, SEQ_DEV, LANES), BF16),
        pltpu.SemaphoreType.DMA((blocks, KINDS)),
    ]
    exchange = functools.partial(lax.all_to_all, axis_name="ctx", split_axis=0, concat_axis=0, tiled=True)

    sent = pl.pallas_call(
        to_channels,
        in_specs=[hbm] * 3,
        out_shape=pltpu.VMEM(pieces.shape, BF16),
        scratch_shapes=turning,
        compiler_params=pltpu.CompilerParams(vmem_limit_bytes=ROOM_BYTES),
        name="to_channels",
    )(*(pltpu.with_memory_space_constraint(x, pltpu.HBM) for x in (signal, filter_taps, upstream)))
    whole = exchange(sent)

    wide, lanes = wide_table(points), lane_table()
    results = pl.pallas_call(
        convolve,
        out_shape=jax.ShapeDtypeStruct((ctx_count, KINDS, SPLITS, groups * PAIR * QUAD, LANES), BF16),
        scratch_shapes=[pltpu.VMEM((groups * CELLS * QUAD, LANES), F32)],
        compiler_params=pltpu.CompilerParams(vmem_limit_bytes=ROOM_BYTES),
        name="convolve",
    )(
        whole,
        skip_gain.reshape(1, chan_count),
        jnp.asarray(wide, BF16),
        jnp.asarray(wide.T / (points * LANES), BF16),
        jnp.asarray(lanes, BF16),
        jnp.asarray(lanes.T, BF16),
        jnp.asarray(twist_tables(points), F32),
    )
    returned = exchange(results)
    return pl.pallas_call(
        to_positions,
        out_specs=[hbm] * 3,
        out_shape=[jax.ShapeDtypeStruct((SEQ_DEV, chan_count), BF16)] * 3,
        scratch_shapes=turning,
        compiler_params=pltpu.CompilerParams(vmem_limit_bytes=ROOM_BYTES),
        name="to_positions",
    )(returned)


def solution(mesh):
    in_specs = (P("ctx", "tp"), P("ctx", "tp"), P("tp"), P("ctx", "tp"))
    out_specs = (P("ctx", "tp"), P("ctx", "tp"), P("ctx", "tp"))
    return jax.shard_map(local, mesh=mesh, in_specs=in_specs, out_specs=out_specs, check_vma=False)
```
